512 devices in a mesh: view: 16 (over y_lo, z), frame: 32 (over y_hi, x, core).
Axes of the slice: x: 4, y: 8 (y_hi: 4, y_lo: 2; y = y_hi * 2 + y_lo), z: 8, core: 2. Of those that a mesh axis runs over, the one named last changes fastest.
Arguments:
- latents: bfloat16 [16, 64, 256, 640], P('view', 'frame'), may hold values from -12 to 12
- norm_gain: float32 [640], replicated, may hold values from 0.25 to 1.75
- qkv_weight: bfloat16 [640, 1920], P('frame'), may hold values from -10 to 10, as said below
- out_weight: bfloat16 [640, 640], P('frame'), may hold values from -0.25 to 0.25
- conv_weight: bfloat16 [3, 640, 640], P(None, 'frame'), may hold values from -0.125 to 0.125
- view_slope: float32 [10], replicated, may hold values from 0.05 to 1.5
Outputs:
- output: bfloat16 [16, 64, 256, 640], P('view', 'frame')
The draws below stay inside these ranges and needn't reach their ends.
Inputs may be any that keep to these rules, and one draw needn't show every extreme that they name: `qkv_weight`: query, key and value columns lie side by side in that order.
All inputs are finite; a program needn't handle non-finite values.
Results may differ from the reference program's by a relative error of at most 0.0095.
Values may be sent and summed in bfloat16 or wider, within the bound.
A program may use at most 128 MiB of HBM per device.

```python
import math
import jax
import jax.numpy as jnp
from jax import lax

C = 640
HEADS = 10
HEAD_DIM = 64
PIX = 256
VIEWS = 16
FRAMES = 64


def draw_latents(key, part):
    key = jax.random.fold_in(key, 5)
    first, second, third = jax.random.split(key, 3)
    shape = (VIEWS, FRAMES, PIX, C)
    noise = jax.random.normal(first, shape, jnp.float32)
    amount = jax.random.normal(second, (VIEWS, FRAMES, PIX, 1), jnp.float32) * 1.5
    shared = jax.random.normal(third, (1, FRAMES, PIX, C), jnp.float32)
    return jnp.clip(noise + amount * shared, -12.0, 12.0).astype(jnp.bfloat16)


def draw_qkv_weight(key, part):
    key = jax.random.fold_in(key, 11)
    first, second = jax.random.split(key, 2)
    base = jax.random.normal(first, (C, 3 * C), jnp.float32) * C ** (-0.5)
    boost = jnp.exp(jax.random.uniform(second, (HEADS,), jnp.float32, 0.7, 1.6))
    boost = jnp.repeat(boost, HEAD_DIM)
    keyed = base[:, C:2 * C] * boost[None, :]
    base = jnp.concatenate([base[:, :C], keyed, base[:, 2 * C:]], axis=1)
    return jnp.clip(base, -10.0, 10.0).astype(jnp.bfloat16)


def levels(key, shape, cuts, least, top_value):
    def one(position, shards_of):
        draws = jax.random.uniform(jax.random.fold_in(jax.random.fold_in(key, 6), position), (shards_of,), jnp.float32, least / len(cuts), top_value / len(cuts))
        return jnp.repeat(jnp.exp(draws), shape[position] // shards_of).reshape((-1,) + (1,) * (len(shape) - position - 1))

    factor_of = one(*cuts[0])
    for cut in cuts[1:]:
        factor_of = factor_of * one(*cut)
    return factor_of


def bell_draw(rng, extent, deviation, most, pieces=(), kind=jnp.bfloat16):
    factor_of = levels(rng, extent, pieces, -0.22, 0.18) if pieces else 1.0
    result = jax.random.normal(rng, extent, jnp.float32) * deviation * factor_of
    return jnp.minimum(jnp.maximum(result, -most), most).astype(kind)


def setup_inputs(seed: int = 0) -> dict:
    key_of = jax.random.split(jax.random.key(seed), 7)
    return {
        "latents": draw_latents(jax.random.fold_in(key_of[6], 71), 0),
        "norm_gain": jnp.clip(1.0 + 0.15 * jax.random.normal(key_of[1], (C,), jnp.float32), 0.25, 1.75),
        "qkv_weight": draw_qkv_weight(jax.random.fold_in(key_of[6], 71), 0),
        "out_weight": bell_draw(key_of[3], (C, C), C ** -0.5, 0.25, ((0, 32),)),
        "conv_weight": bell_draw(key_of[4], (3, C, C), (3 * C) ** -0.5, 0.125, ((1, 32),)),
        "view_slope": jnp.clip(jnp.exp(jax.random.uniform(key_of[5], (HEADS,), jnp.float32, math.log(0.05), math.log(1.5))), 0.05, 1.5),
    }


def reference(latents, norm_gain, qkv_weight, out_weight, conv_weight, view_slope):
    wide = latents.astype(jnp.float32)
    normed = (wide * jax.lax.rsqrt(lax.optimization_barrier(jnp.mean(wide * wide, axis=-1, keepdims=True)) + 1e-06) * norm_gain).astype(jnp.bfloat16)
    qkv = jnp.einsum('vfpc,cd->vfpd', normed.astype(jnp.float32), qkv_weight.astype(jnp.float32)).astype(jnp.bfloat16)
    shape = (VIEWS, FRAMES, PIX, HEADS, HEAD_DIM)
    query = qkv[..., :C].reshape(shape).astype(jnp.float32)
    keys = qkv[..., C:2 * C].reshape(shape).astype(jnp.float32)
    values = qkv[..., 2 * C:].reshape(shape).astype(jnp.float32)
    order = jnp.arange(VIEWS, dtype=jnp.int32)
    gap = jnp.abs(order[:, None] - order[None, :])
    dist = jnp.minimum(gap, VIEWS - gap).astype(jnp.float32)
    scores = jnp.einsum('afphd,bfphd->fphab', query, keys) * (1.0 / HEAD_DIM ** 0.5)
    scores = scores - view_slope[:, None, None] * dist
    weights = jax.nn.softmax(scores, axis=-1).astype(jnp.bfloat16)
    mixed = jnp.einsum('fphab,bfphd->afphd', weights.astype(jnp.float32), values).astype(jnp.bfloat16)
    mixed = mixed.reshape(VIEWS, FRAMES, PIX, C)
    hidden = (wide + jnp.einsum('vfpc,cd->vfpd', mixed.astype(jnp.float32), out_weight.astype(jnp.float32))).astype(jnp.bfloat16)
    padded = jnp.pad(hidden, ((0, 0), (1, 1), (0, 0), (0, 0))).astype(jnp.float32)
    total = hidden.astype(jnp.float32)
    for tap in range(3):
        total = total + jnp.einsum('vfpc,cd->vfpd', padded[:, tap:tap + FRAMES], conv_weight[tap].astype(jnp.float32))
    return total.astype(jnp.bfloat16)
```

```python
import functools

import jax
import jax.numpy as jnp
from jax import lax
from jax.experimental import pallas as pl
from jax.experimental.pallas import tpu as pltpu
from jax.sharding import PartitionSpec as P

ZS, YLS, XS, YHS = 8, 2, 4, 4
VIEWS, PIX, C, HEADS = 16, 256, 640, 10
ROWS = 80
QW, OW = 512, 640
PEERS = [(dy, dz) for dz in (4, 3, 5, 2, 6, 1, 7, 0) for dy in (0, 1) if (dy, dz) != (0, 0)]
XSTEPS = (1, -1, 2)
XFROM = (3, 1, 2)
ORDER = (0, 1, 3, 2)
BF, F32 = jnp.bfloat16, jnp.float32


class Place:
    def __init__(self):
        v, f = lax.axis_index("view"), lax.axis_index("frame")
        self.view, self.frame = v, f
        self.yl, self.z = v // ZS, v % ZS
        self.yh, self.x, self.core = f // (XS * 2), (f // 2) % XS, f % 2
        self.even = self.yl == 0
        self.odd = self.yl == 1

    def at(self, yl, z, yh, x, core):
        return (yl * ZS + z, yh * (XS * 2) + x * 2 + core)

    def x_peer(self, d):
        return (self.view, self.yh * (XS * 2) + ((self.x + d + XS) % XS) * 2 + self.core)

    def y_peer(self, d):
        y = (self.yh * 2 + self.yl + d + 8) % 8
        return self.at(y % 2, self.z, y // 2, self.x, self.core)

    def sibling(self):
        return (self.view, self.yh * (XS * 2) + self.x * 2 + 1 - self.core)

    def frame_peer(self, d):
        return (self.view, (self.frame + d + 32) % 32)

    def view_peer(self, dy, dz):
        view = ((self.yl + dy) % YLS) * ZS + (self.z + dz) % ZS
        return view, (view, self.frame)


def remote(src, dst, send, recv, device):
    return pltpu.make_async_remote_copy(
        src_ref=src, dst_ref=dst, send_sem=send, recv_sem=recv,
        device_id=device, device_id_type=pl.DeviceIdType.MESH,
    )


class GatherXY:
    def __init__(self, here, buf, stride, off, n, sems):
        self.h, self.buf, self.stride, self.off, self.n = here, buf, stride, off, n
        (self.xs, self.xr, self.rs, self.rr, self.ls, self.lr, self.ss, self.sr) = sems

    def piece(self, b, rel):
        h = self.h
        row = pl.multiple_of(((b % YHS) * 2 + h.core) * ROWS, 16)
        col = pl.multiple_of(((h.x + rel) % XS) * self.stride + self.off, 128)
        return self.buf.at[pl.ds(row, ROWS), pl.ds(col, self.n)]

    def copy(self, b, rel, send, recv, device):
        p = self.piece(b, rel)
        return remote(p, p, send, recv, device)

    def to_sibling(self, b, rel):
        i = (b % YHS) * XS + (self.h.x + rel) % XS
        self.copy(b, rel, self.ss.at[i], self.sr.at[i], self.h.sibling()).start()

    def right(self, i, b, rel):
        return self.copy(b, rel, self.rs.at[i], self.rr.at[i], self.h.y_peer(1))

    def left(self, i, b, rel):
        return self.copy(b, rel, self.ls.at[i], self.lr.at[i], self.h.y_peer(-1))

    def steps(self):
        h = self.h
        for i, d in enumerate(XSTEPS):
            self.copy(h.yh, 0, self.xs.at[i], self.xr.at[i], h.x_peer(d)).start()
        for p, rel in enumerate(ORDER):
            if p:
                i = XFROM.index(rel)
                self.copy(h.yh, rel, self.xs.at[i], self.xr.at[i], h.x_peer(1)).wait_recv()

            @pl.when(h.odd)
            def _():
                self.right(p, h.yh, rel).start()

            @pl.when(h.even)
            def _():
                self.left(p, h.yh, rel).start()

            self.to_sibling(h.yh, rel)
            if p == 0:
                yield
        yield
        for i in range(6):
            far = i >= 4
            rel = ORDER[i - 4] if far else ORDER[i]
            b = h.yh + (2 if far else 3)
            self.right(i, b, rel).wait_recv()

            @pl.when(h.even)
            def _():
                self.right(i, b, rel).start()

            if i < 2:
                @pl.when(h.odd)
                def _():
                    self.right(4 + i, b, rel).start()

            self.to_sibling(b, rel)

            rel = ORDER[i - 2] if far else ORDER[i]
            b = h.yh + (2 if far else 1)
            self.left(i, b, rel).wait_recv()

            @pl.when(h.odd)
            def _():
                self.left(i, b, rel).start()

            if 2 <= i < 4:
                @pl.when(h.even)
                def _():
                    self.left(2 + i, b, rel).start()

            self.to_sibling(b, rel)
            yield

    def arrive(self):
        for i in range(16):
            self.copy(0, 0, self.ss.at[i], self.sr.at[i], self.h.sibling()).wait_recv()

    def drain(self):
        for sem, count in ((self.xs, 3), (self.rs, 6), (self.ls, 6), (self.ss, 16)):
            for i in range(count):
                self.copy(0, 0, sem.at[i], self.xr.at[0], self.h.sibling()).wait_send()

    @staticmethod
    def sems():
        return [pltpu.SemaphoreType.DMA((k,)) for k in (3, 3, 6, 6, 6, 6, 16, 16)]


class GatherYX:
    def __init__(self, here, buf, stride, off, n, first, sems):
        self.h, self.buf, self.stride, self.off, self.n = here, buf, stride, off, n
        self.first = first
        (self.rs, self.rr, self.ls, self.lr, self.xs, self.xr, self.ss, self.sr) = sems

    def piece(self, b, rel, part=0):
        h = self.h
        row = pl.multiple_of(((b % YHS) * 2 + h.core) * ROWS, 16)
        off = self.off + (self.first if part == 2 else 0)
        n = (self.n, self.first, self.n - self.first)[part]
        col = pl.multiple_of(((h.x + rel) % XS) * self.stride + off, 128)
        return self.buf.at[pl.ds(row, ROWS), pl.ds(col, n)]

    def copy(self, b, rel, send, recv, device, part=0):
        p = self.piece(b, rel, part)
        return remote(p, p, send, recv, device)

    def to_sibling(self, b, rel):
        i = (b % YHS) * XS + (self.h.x + rel) % XS
        self.copy(b, rel, self.ss.at[i], self.sr.at[i], self.h.sibling()).start()

    def right(self, i, b):
        part = 1 if i else 0
        return self.copy(b, 0, self.rs.at[i], self.rr.at[i], self.h.y_peer(1), part)

    def left(self, i, b):
        part = 2 if i else 0
        return self.copy(b, 0, self.ls.at[i], self.lr.at[i], self.h.y_peer(-1), part)

    def across(self, j, b):
        for i, d in enumerate(XSTEPS):
            k = j * 3 + i
            self.copy(b, 0, self.xs.at[k], self.xr.at[k], self.h.x_peer(d)).start()
        self.to_sibling(b, 0)

    def steps(self):
        h = self.h

        @pl.when(h.odd)
        def _():
            self.right(0, h.yh).start()

        @pl.when(h.even)
        def _():
            self.left(0, h.yh).start()

        self.across(0, h.yh)
        yield
        b = h.yh + 3
        self.right(0, b).wait_recv()

        @pl.when(h.even)
        def _():
            self.right(0, b).start()

        @pl.when(h.odd)
        def _():
            self.right(1, b).start()

        self.across(1, b)
        b = h.yh + 1
        self.left(0, b).wait_recv()

        @pl.when(h.odd)
        def _():
            self.left(0, b).start()

        @pl.when(h.even)
        def _():
            self.left(1, b).start()

        self.across(2, b)
        yield
        b = h.yh + 2
        self.right(1, b).wait_recv()

        @pl.when(h.even)
        def _():
            self.right(1, b).start()

        self.left(1, b).wait_recv()

        @pl.when(h.odd)
        def _():
            self.left(1, b).start()

        self.across(3, b)
        yield
        for j, step in enumerate((0, 3, 1, 2)):
            for i, rel in enumerate(XFROM):
                k = j * 3 + i
                self.copy(h.yh + step, rel, self.xs.at[k], self.xr.at[k], h.x_peer(1)).wait_recv()
                self.to_sibling(h.yh + step, rel)
            yield

    def arrive(self):
        for i in range(16):
            self.copy(0, 0, self.ss.at[i], self.sr.at[i], self.h.sibling()).wait_recv()

    def drain(self):
        for i in range(2):
            self.right(i, 0).wait_send()
            self.left(i, 0).wait_send()
        for sem, count in ((self.xs, 12), (self.ss, 16)):
            for i in range(count):
                self.copy(0, 0, sem.at[i], self.xr.at[0], self.h.sibling()).wait_send()

    @staticmethod
    def sems():
        return [pltpu.SemaphoreType.DMA((k,)) for k in (2, 2, 2, 2, 12, 12, 16, 16)]


def advance(*generators, times=1):
    for _ in range(times):
        for g in generators:
            next(g, None)


def kernel(
    lat, gain, qsh, osh, csh, slope, out,
    pieces, xin, outb, back, dist, wq, wo, sq, so, r1q, r1o, r32, qkv, mix, hid,
    hsend, hleft, hright,
    in_s, in_r, out_s, out_r, halo_s, halo_r, s1_s, s1_r, *sems,
):
    h = Place()
    barrier = pltpu.get_barrier_semaphore()
    partners = [h.view_peer(*p)[1] for p in PEERS]
    for dx in range(XS):
        for dc in range(2):
            if dx or dc:
                partners.append(
                    (h.view, h.yh * 8 + ((h.x + dx) % XS) * 2 + (h.core + dc) % 2)
                )
    partners += [h.y_peer(1), h.y_peer(-1), h.frame_peer(1), h.frame_peer(-1)]
    for p in partners:
        pl.semaphore_signal(barrier, inc=1, device_id=p, device_id_type=pl.DeviceIdType.MESH)

    sq[...] = jnp.zeros_like(sq)
    so[...] = jnp.zeros_like(so)
    sq[0:20, 0:1920] = qsh[...]
    so[0:20, 0:640] = osh[...]
    for t in range(3):
        so[0:20, 640 * (t + 1) : 640 * (t + 2)] = csh[t]
    both = [lat[0, f].astype(F32).reshape(32, 8, C) for f in range(2)]
    pieces[...] = jnp.stack(both, axis=1).reshape(32, 16, C).astype(BF)
    row = lax.broadcasted_iota(jnp.int32, (256, 256), 0)
    col = lax.broadcasted_iota(jnp.int32, (256, 256), 1)
    gap = jnp.abs(row // 16 - col // 16)
    gap = jnp.minimum(gap, VIEWS - gap).astype(F32)
    dist[...] = jnp.where(row % 16 == col % 16, gap, 1e30)

    pl.semaphore_wait(barrier, len(partners))

    half = h.x // 2
    slot = (h.x % 2) * 2 + h.core
    stages = ((sq, r1q, QW), (so, r1o, OW))

    def shard(t, x):
        src, dst, width = stages[t]
        device = (h.view, h.yh * 8 + x * 2 + half)
        return remote(
            src.at[:, pl.ds(x * width, width)], dst.at[slot], s1_s.at[t, x], s1_r.at[t, slot], device
        )

    mine = half == h.core
    for t in range(2):
        for x in range(XS):
            src, dst, width = stages[t]

            @pl.when(jnp.logical_not(mine & (h.x == x)))
            def _():
                shard(t, x).start()

            @pl.when(mine & (h.x == x))
            def _():
                pltpu.make_async_copy(
                    src.at[:, pl.ds(x * width, width)], dst.at[slot], s1_r.at[t, slot]
                ).start()

    def send_in(c, i):
        v, device = h.view_peer(*PEERS[i])
        return remote(
            pieces.at[v * 2 + c], xin.at[c, h.view], in_s.at[c, i], in_r.at[c, i], device
        )

    for c in range(2):
        for i in range(15):
            send_in(c, i).start()
        xin[c, h.view] = pieces[h.view * 2 + c]

    def put_together(t):
        src, dst, width = stages[t]
        for s in range(4):
            pltpu.make_async_copy(dst.at[s], dst.at[s], s1_r.at[t, s]).wait()
            r32[20 * s : 20 * s + 20, 0:width] = dst[s, 0:20, :].astype(F32)
        buf = (wq, wo)[t]
        rows = pl.multiple_of((h.yh * 2 + h.core) * ROWS, 16)
        cols = pl.multiple_of(h.x * width, 128)
        buf[pl.ds(rows, ROWS), pl.ds(cols, width)] = r32[:, 0:width].astype(BF)

    qa = GatherXY(h, wq, QW, 0, 256, sems[0:8])
    qb = GatherYX(h, wq, QW, 256, 256, 128, sems[8:16])
    oa = GatherXY(h, wo, OW, 0, 384, sems[16:24])
    ob = GatherYX(h, wo, OW, 384, 256, 128, sems[24:32])
    sqa, sqb, soa, sob = qa.steps(), qb.steps(), oa.steps(), ob.steps()

    put_together(0)
    advance(sqa, sqb, times=2)
    put_together(1)
    advance(sqa, sqb, times=3)
    advance(soa, sob)
    advance(sqa, sqb, times=8)
    qa.arrive()
    qb.arrive()

    def project(c):
        for i in range(15):
            send_in(c, i).wait_recv()
        wide = xin[c].reshape(256, C).astype(F32)
        scale = lax.rsqrt(jnp.mean(wide * wide, axis=-1, keepdims=True) + 1e-06)
        normed = (wide * scale * gain[...]).astype(BF)
        for t in range(5):
            qkv[c, :, 384 * t : 384 * (t + 1)] = jnp.dot(
                normed, wq[:, 384 * t : 384 * (t + 1)], preferred_element_type=F32
            ).astype(BF)

    low = lax.broadcasted_iota(jnp.int32, (256, 128), 1) < 64

    def attend(c, s):
        q = qkv[c, :, 128 * s : 128 * (s + 1)]
        k = qkv[c, :, 640 + 128 * s : 640 + 128 * (s + 1)]
        v = qkv[c, :, 1280 + 128 * s : 1280 + 128 * (s + 1)]
        v = jnp.concatenate([v, jnp.ones_like(v)], axis=1)
        parts = []
        for e in range(2):
            qe = jnp.where(low if e == 0 else jnp.logical_not(low), q, jnp.zeros_like(q))
            scores = lax.dot_general(
                qe, k, (((1,), (1,)), ((), ())), preferred_element_type=F32
            )
            scores = scores * 0.125 - slope[2 * s + e] * dist[...]
            top = jnp.max(scores, axis=-1, keepdims=True)
            weights = jnp.exp(scores - top).astype(BF)
            o = jnp.dot(weights, v, preferred_element_type=F32)
            parts.append(o[:, 0:128] / o[:, 128:256])
        mix[c, :, 128 * s : 128 * (s + 1)] = jnp.where(low, parts[0], parts[1]).astype(BF)

    def halo(c, side):
        dst = (hright, hleft)[side]
        return remote(
            hsend.at[c, side], dst.at[c], halo_s.at[c, side], halo_r.at[c, side],
            h.frame_peer((-1, 1)[side]),
        )

    def add(c):
        wide = xin[c].reshape(256, C).astype(F32)
        total = wide + jnp.dot(mix[c], wo[:, 0:640], preferred_element_type=F32)
        hidden = total.astype(BF)
        hid[c] = hidden
        split = hidden.astype(F32).reshape(16, 2, 8, C)
        for side in range(2):
            hsend[c, side] = split[:, side].reshape(128, C).astype(BF)
            halo(c, side).start()

    def convolve(c):
        for side in range(2):
            halo(c, side).wait_recv()
        wide = hid[c].astype(F32)
        split = wide.reshape(16, 2, 8, C)
        before = hleft[c].astype(F32).reshape(16, 8, C)
        after = hright[c].astype(F32).reshape(16, 8, C)
        before = jnp.where(h.frame == 0, 0.0, before)
        after = jnp.where(h.frame == 31, 0.0, after)
        taps = (
            jnp.stack([before, split[:, 0]], axis=1).reshape(256, C).astype(BF),
            hid[c],
            jnp.stack([split[:, 1], after], axis=1).reshape(256, C).astype(BF),
        )
        for t in range(3):
            wide = wide + jnp.dot(
                taps[t], wo[:, 640 * (t + 1) : 640 * (t + 2)], preferred_element_type=F32
            )
        outb[c] = wide.astype(BF).reshape(16, 16, C)
        for i in range(15):
            send_out(c, i).start()
        back[c, h.view] = outb[c, h.view]

    def send_out(c, i):
        v, device = h.view_peer(*PEERS[i])
        return remote(
            outb.at[c, v], back.at[c, h.view], out_s.at[c, i], out_r.at[c, i], device
        )

    project(0)
    advance(soa, sob)
    for s in range(5):
        attend(0, s)
        advance(soa, sob)
    advance(soa, sob, times=8)
    oa.arrive()
    ob.arrive()
    add(0)
    project(1)
    attend(1, 0)
    attend(1, 1)
    convolve(0)
    for s in range(2, 5):
        attend(1, s)
    add(1)
    convolve(1)

    for g in (qa, qb, oa, ob):
        g.drain()
    for t in range(2):
        for x in range(XS):
            @pl.when(jnp.logical_not(mine & (h.x == x)))
            def _():
                shard(t, x).wait_send()
    for c in range(2):
        for side in range(2):
            halo(c, side).wait_send()
        for i in range(15):
            send_in(c, i).wait_send()
    for c in range(2):
        for i in range(15):
            send_out(c, i).wait_recv()
    both = [back[c].astype(F32).reshape(16, 2, 8, C) for c in range(2)]
    for f in range(2):
        out[0, f] = jnp.stack([b[:, f] for b in both], axis=1).reshape(PIX, C).astype(BF)
    for c in range(2):
        for i in range(15):
            send_out(c, i).wait_send()


def per_device(latents, norm_gain, qkv_weight, out_weight, conv_weight, view_slope):
    vmem = pl.BlockSpec(memory_space=pltpu.VMEM)
    dma = pltpu.SemaphoreType.DMA
    scratch = [
        pltpu.VMEM((32, 16, C), BF),
        pltpu.VMEM((2, 16, 16, C), BF),
        pltpu.VMEM((2, 16, 16, C), BF),
        pltpu.VMEM((2, 16, 16, C), BF),
        pltpu.VMEM((256, 256), F32),
        pltpu.VMEM((C, 4 * QW), BF),
        pltpu.VMEM((C, 4 * OW), BF),
        pltpu.VMEM((32, 4 * QW), BF),
        pltpu.VMEM((32, 4 * OW), BF),
        pltpu.VMEM((4, 32, QW), BF),
        pltpu.VMEM((4, 32, OW), BF),
        pltpu.VMEM((ROWS, OW), F32),
        pltpu.VMEM((2, 256, 3 * C), BF),
        pltpu.VMEM((2, 256, C), BF),
        pltpu.VMEM((2, 256, C), BF),
        pltpu.VMEM((2, 2, 128, C), BF),
        pltpu.VMEM((2, 128, C), BF),
        pltpu.VMEM((2, 128, C), BF),
        dma((2, 15)), dma((2, 15)), dma((2, 15)), dma((2, 15)),
        dma((2, 2)), dma((2, 2)), dma((2, 4)), dma((2, 4)),
    ]
    scratch += GatherXY.sems() + GatherYX.sems() + GatherXY.sems() + GatherYX.sems()
    return pl.pallas_call(
        kernel,
        out_shape=jax.ShapeDtypeStruct(latents.shape, latents.dtype),
        in_specs=[vmem] * 5 + [pl.BlockSpec(memory_space=pltpu.SMEM)],
        out_specs=vmem,
        scratch_shapes=scratch,
        compiler_params=pltpu.CompilerParams(
            collective_id=0, has_side_effects=True, vmem_limit_bytes=56 * 1024 * 1024
        ),
        cost_estimate=pl.CostEstimate(
            flops=4 * 10**9, bytes_accessed=2 * 10**6, transcendentals=10**6
        ),
    )(latents, norm_gain.reshape(1, C), qkv_weight, out_weight, conv_weight, view_slope)


def solution(mesh):
    in_specs = (
        P("view", "frame", None, None),
        P(),
        P("frame", None),
        P("frame", None),
        P(None, "frame", None),
        P(),
    )
    return jax.shard_map(
        per_device,
        mesh=mesh,
        in_specs=in_specs,
        out_specs=P("view", "frame", None, None),
        check_vma=False,
    )
```

```python
import jax
import jax.numpy as jnp
from jax import lax
from jax.experimental import pallas as pl
from jax.experimental.pallas import tpu as pltpu
from jax.sharding import PartitionSpec as P

ZS, YLS, XS, YHS = 8, 2, 4, 4
VIEWS, PIX, C, HEADS = 16, 256, 640, 10
ROWS = 80
QA, OA, GROUP = 1024, 384, 384
PEERS = [(dy, dz) for dz in (4, 3, 5, 2, 6, 1, 7, 0) for dy in (0, 1) if (dy, dz) != (0, 0)]
XSTEPS = (1, -1, 2)
XFROM = (3, 1, 2)
BF, F32 = jnp.bfloat16, jnp.float32


class Place:
    def __init__(self):
        v, f = lax.axis_index("view"), lax.axis_index("frame")
        self.view, self.frame = v, f
        self.yl, self.z = v // ZS, v % ZS
        self.yh, self.x, self.core = f // (XS * 2), (f // 2) % XS, f % 2
        self.even = self.yl == 0
        self.odd = self.yl == 1

    def at(self, yl, z, yh, x, core):
        return (yl * ZS + z, yh * (XS * 2) + x * 2 + core)

    def x_peer(self, d):
        return (self.view, self.yh * (XS * 2) + ((self.x + d + XS) % XS) * 2 + self.core)

    def y_peer(self, d):
        y = (self.yh * 2 + self.yl + d + 8) % 8
        return self.at(y % 2, self.z, y // 2, self.x, self.core)

    def sibling(self):
        return (self.view, self.yh * (XS * 2) + self.x * 2 + 1 - self.core)

    def frame_peer(self, d):
        return (self.view, (self.frame + d + 32) % 32)

    def view_peer(self, dy, dz):
        view = ((self.yl + dy) % YLS) * ZS + (self.z + dz) % ZS
        return view, (view, self.frame)


def remote(src, dst, send, recv, device):
    return pltpu.make_async_remote_copy(
        src_ref=src, dst_ref=dst, send_sem=send, recv_sem=recv,
        device_id=device, device_id_type=pl.DeviceIdType.MESH,
    )


class Gather:
    def __init__(self, here, buf, across, sems):
        self.h, self.buf, self.across = here, buf, across
        self.count = buf.shape[0]
        self.side = 2 * here.yl - 1
        (self.ys, self.yr, self.xs, self.xr, self.ss, self.sr) = sems

    def piece(self, b, p):
        row = pl.multiple_of((((b + 8) % YHS) * 2 + self.h.core) * ROWS, 16)
        return self.buf.at[p, pl.ds(row, ROWS)]

    def copy(self, b, p, send, recv, device):
        ref = self.piece(b, p)
        return remote(ref, ref, send, recv, device)

    def hop(self, k, i, b, p):
        d = (self.side, -self.side, self.side)[k]
        return self.copy(b, p, self.ys.at[k, i], self.yr.at[k, i], self.h.y_peer(d))

    def to_sibling(self, b, p):
        i = ((b + 8) % YHS) * self.count + p
        self.copy(b, p, self.ss.at[i], self.sr.at[i], self.h.sibling()).start()

    def pass_on(self, k, b, p):
        if self.across:
            for i, d in enumerate(XSTEPS):
                i += 3 * k
                self.copy(b, p, self.xs.at[i], self.xr.at[i], self.h.x_peer(d)).start()
        self.to_sibling(b, p)

    def steps(self):
        h = self.h
        own = [h.x] if self.across else range(self.count)
        blocks = (h.yh + self.side, h.yh - self.side, h.yh + 2)
        for i, p in enumerate(own):
            self.hop(0, i, h.yh, p).start()
        for p in own:
            self.pass_on(0, h.yh, p)
        yield
        for k in range(3):
            for i, p in enumerate(own):
                self.hop(k, i, blocks[k], p).wait_recv()
                if k < 2:
                    self.hop(k + 1, i, blocks[k], p).start()
                self.pass_on(k + 1, blocks[k], p)
            yield
        if self.across:
            for k, b in enumerate((h.yh,) + blocks):
                for i, rel in enumerate(XFROM):
                    p = (h.x + rel) % XS
                    i += 3 * k
                    self.copy(b, p, self.xs.at[i], self.xr.at[i], h.x_peer(1)).wait_recv()
                    self.to_sibling(b, p)
                yield

    def arrive(self):
        for i in range(YHS * self.count):
            self.copy(0, 0, self.ss.at[i], self.sr.at[i], self.h.sibling()).wait_recv()

    def drain(self):
        own = 1 if self.across else self.count
        waits = [self.ys.at[k, i] for k in range(3) for i in range(own)]
        waits += [self.ss.at[i] for i in range(YHS * self.count)]
        if self.across:
            waits += [self.xs.at[i] for i in range(12)]
        for sem in waits:
            self.copy(0, 0, sem, self.sr.at[0], self.h.sibling()).wait_send()

    @staticmethod
    def sems(count, across):
        own = 1 if across else count
        shapes = ((3, own), (3, own), (12,), (12,), (YHS * count,), (YHS * count,))
        return [pltpu.SemaphoreType.DMA(k) for k in shapes]


def advance(*generators, times=1):
    for _ in range(times):
        for g in generators:
            next(g, None)


def kernel(
    lat, gain, qsh, osh, csh, slope, out,
    pieces, xin, outb, back, dist, wqa, wqb, woa, wob, sq, so, r1q, r1o, r32, qkv, mix, hid,
    hsend, hleft, hright,
    in_s, in_r, out_s, out_r, halo_s, halo_r, s1_s, s1_r, *sems,
):
    h = Place()
    barrier = pltpu.get_barrier_semaphore()
    partners = [h.view_peer(*p)[1] for p in PEERS]
    for dx in range(XS):
        for dc in range(2):
            if dx or dc:
                partners.append(
                    (h.view, h.yh * 8 + ((h.x + dx) % XS) * 2 + (h.core + dc) % 2)
                )
    partners += [h.y_peer(1), h.y_peer(-1), h.frame_peer(1), h.frame_peer(-1)]
    for p in partners:
        pl.semaphore_signal(barrier, inc=1, device_id=p, device_id_type=pl.DeviceIdType.MESH)

    for x in range(XS):
        first, last = QA + GROUP * x, QA + GROUP * (x + 1)
        sq[x, 0:20, 0:QA] = qsh[:, 0:QA]
        if first < 1920:
            sq[x, 0:20, QA : QA + min(last, 1920) - first] = qsh[:, first : min(last, 1920)]
        if last > 1920:
            skip = max(first, 1920)
            sq[x, 0:20, QA + skip - first :] = osh[:, skip - 1920 : last - 1920]
        so[x, 0:20, 0:OA] = csh[0, :, 0:OA]
        at, end = OA + GROUP * x, OA + GROUP * (x + 1)
        while at < end:
            t = at // C
            stop = min(end, C * (t + 1))
            to = OA + at - (OA + GROUP * x)
            so[x, 0:20, to : to + stop - at] = csh[t, :, at - C * t : stop - C * t]
            at = stop
        sq[x, 20:32, :] = jnp.zeros((12, QA + GROUP), BF)
        so[x, 20:32, :] = jnp.zeros((12, OA + GROUP), BF)
    both = [lat[0, f].astype(F32).reshape(32, 8, C) for f in range(2)]
    pieces[...] = jnp.stack(both, axis=1).reshape(32, 16, C).astype(BF)
    row = lax.broadcasted_iota(jnp.int32, (256, 256), 0)
    col = lax.broadcasted_iota(jnp.int32, (256, 256), 1)
    gap = jnp.abs(row // 16 - col // 16)
    gap = jnp.minimum(gap, VIEWS - gap).astype(F32)
    dist[...] = jnp.where(row % 16 == col % 16, gap, 1e30)

    pl.semaphore_wait(barrier, len(partners))

    half = h.x // 2
    slot = (h.x % 2) * 2 + h.core
    stages = ((sq, r1q, QA + GROUP), (so, r1o, OA + GROUP))

    def shard(t, x):
        src, dst = stages[t][:2]
        device = (h.view, h.yh * 8 + x * 2 + half)
        return remote(
            src.at[x], dst.at[slot], s1_s.at[t, x], s1_r.at[t, slot], device
        )

    mine = half == h.core
    for t in range(2):
        for x in range(XS):
            src, dst = stages[t][:2]

            @pl.when(jnp.logical_not(mine & (h.x == x)))
            def _():
                shard(t, x).start()

            @pl.when(mine & (h.x == x))
            def _():
                pltpu.make_async_copy(src.at[x], dst.at[slot], s1_r.at[t, slot]).start()

    def send_in(c, i):
        v, device = h.view_peer(*PEERS[i])
        return remote(
            pieces.at[v * 2 + c], xin.at[c, h.view], in_s.at[c, i], in_r.at[c, i], device
        )

    for c in range(2):
        for i in range(15):
            send_in(c, i).start()
        xin[c, h.view] = pieces[h.view * 2 + c]

    def put_together(t):
        dst, width = stages[t][1:]
        for s in range(4):
            pltpu.make_async_copy(dst.at[s], dst.at[s], s1_r.at[t, s]).wait()
            r32[20 * s : 20 * s + 20, 0:width] = dst[s, 0:20, :].astype(F32)
        rows = pl.ds(pl.multiple_of((h.yh * 2 + h.core) * ROWS, 16), ROWS)
        a, b = ((wqa, wqb), (woa, wob))[t]
        n = a.shape[2]
        for p in range(a.shape[0]):
            a[p, rows] = r32[:, n * p : n * (p + 1)].astype(BF)
        b[h.x, rows] = r32[:, width - GROUP : width].astype(BF)

    qa = Gather(h, wqa, False, sems[0:6])
    qb = Gather(h, wqb, True, sems[6:12])
    oa = Gather(h, woa, False, sems[12:18])
    ob = Gather(h, wob, True, sems[18:24])
    sqa, sqb, soa, sob = qa.steps(), qb.steps(), oa.steps(), ob.steps()

    put_together(0)
    advance(sqb, sqa)
    put_together(1)
    advance(sqb, sqa, times=2)
    advance(sob, soa)
    advance(sqb, sqa)
    advance(sqb, times=4)
    qa.arrive()
    qb.arrive()

    def project(c):
        for i in range(15):
            send_in(c, i).wait_recv()
        wide = xin[c].reshape(256, C).astype(F32)
        scale = lax.rsqrt(jnp.mean(wide * wide, axis=-1, keepdims=True) + 1e-06)
        normed = (wide * scale * gain[...].reshape(1, C)).astype(BF)
        tiles = [(256 * p, wqa[p]) for p in range(4)]
        tiles += [(1024, wqb[0]), (1408, wqb[1]), (1792, wqb[2, :, 0:128])]
        for at, w in tiles:
            qkv[c, :, at : at + w.shape[1]] = jnp.dot(
                normed, w, preferred_element_type=F32
            ).astype(BF)

    low = lax.broadcasted_iota(jnp.int32, (256, 128), 1) < 64

    def attend(c, s):
        q = qkv[c, :, 128 * s : 128 * (s + 1)]
        k = qkv[c, :, 640 + 128 * s : 640 + 128 * (s + 1)]
        v = qkv[c, :, 1280 + 128 * s : 1280 + 128 * (s + 1)]
        v = jnp.concatenate([v, jnp.ones_like(v)], axis=1)
        parts = []
        for e in range(2):
            qe = jnp.where(low if e == 0 else jnp.logical_not(low), q, jnp.zeros_like(q))
            scores = lax.dot_general(
                qe, k, (((1,), (1,)), ((), ())), preferred_element_type=F32
            )
            scores = scores * 0.125 - slope[2 * s + e] * dist[...]
            top = jnp.max(scores, axis=-1, keepdims=True)
            weights = jnp.exp(scores - top).astype(BF)
            o = jnp.dot(weights, v, preferred_element_type=F32)
            parts.append(o[:, 0:128] / o[:, 128:256])
        mix[c, :, 128 * s : 128 * (s + 1)] = jnp.where(low, parts[0], parts[1]).astype(BF)

    def halo(c, side):
        dst = (hright, hleft)[side]
        return remote(
            hsend.at[c, side], dst.at[c], halo_s.at[c, side], halo_r.at[c, side],
            h.frame_peer((-1, 1)[side]),
        )

    taps_of = (
        lambda: (woa[0], wob[0, :, 0:256]),
        lambda: (wob[0, :, 256:384], wob[1], wob[2, :, 0:128]),
        lambda: (wob[2, :, 128:384], wob[3]),
        lambda: (wqb[2, :, 128:384], wqb[3]),
    )

    def times(a, t):
        return jnp.concatenate(
            [jnp.dot(a, w, preferred_element_type=F32) for w in taps_of[t]()], axis=1
        )

    def add(c):
        wide = xin[c].reshape(256, C).astype(F32)
        hidden = (wide + times(mix[c], 3)).astype(BF)
        hid[c] = hidden
        split = hidden.astype(F32).reshape(16, 2, 8, C)
        for side in range(2):
            hsend[c, side] = split[:, side].reshape(128, C).astype(BF)
            halo(c, side).start()

    def convolve(c):
        for side in range(2):
            halo(c, side).wait_recv()
        wide = hid[c].astype(F32)
        split = wide.reshape(16, 2, 8, C)
        before = hleft[c].astype(F32).reshape(16, 8, C)
        after = hright[c].astype(F32).reshape(16, 8, C)
        before = jnp.where(h.frame == 0, 0.0, before)
        after = jnp.where(h.frame == 31, 0.0, after)
        taps = (
            jnp.stack([before, split[:, 0]], axis=1).reshape(256, C).astype(BF),
            hid[c],
            jnp.stack([split[:, 1], after], axis=1).reshape(256, C).astype(BF),
        )
        for t in range(3):
            wide = wide + times(taps[t], t)
        outb[c] = wide.astype(BF).reshape(16, 16, C)
        for i in range(15):
            send_out(c, i).start()
        back[c, h.view] = outb[c, h.view]

    def send_out(c, i):
        v, device = h.view_peer(*PEERS[i])
        return remote(
            outb.at[c, v], back.at[c, h.view], out_s.at[c, i], out_r.at[c, i], device
        )

    project(0)
    advance(sob, soa)
    for k in range(5):
        attend(0, k)
    add(0)
    advance(sob, soa)
    project(1)
    for k in range(5):
        attend(1, k)
    add(1)
    advance(sob, soa)
    advance(sob, times=4)
    oa.arrive()
    ob.arrive()
    convolve(0)
    convolve(1)

    for g in (qa, qb, oa, ob):
        g.drain()
    for t in range(2):
        for x in range(XS):
            @pl.when(jnp.logical_not(mine & (h.x == x)))
            def _():
                shard(t, x).wait_send()
    for c in range(2):
        for side in range(2):
            halo(c, side).wait_send()
        for i in range(15):
            send_in(c, i).wait_send()
    for c in range(2):
        for i in range(15):
            send_out(c, i).wait_recv()
    both = [back[c].astype(F32).reshape(16, 2, 8, C) for c in range(2)]
    for f in range(2):
        out[0, f] = jnp.stack([b[:, f] for b in both], axis=1).reshape(PIX, C).astype(BF)
    for c in range(2):
        for i in range(15):
            send_out(c, i).wait_send()


def per_device(latents, norm_gain, qkv_weight, out_weight, conv_weight, view_slope):
    vmem = pl.BlockSpec(memory_space=pltpu.VMEM)
    dma = pltpu.SemaphoreType.DMA
    scratch = [
        pltpu.VMEM((32, 16, C), BF),
        pltpu.VMEM((2, 16, 16, C), BF),
        pltpu.VMEM((2, 16, 16, C), BF),
        pltpu.VMEM((2, 16, 16, C), BF),
        pltpu.VMEM((256, 256), F32),
        pltpu.VMEM((4, C, QA // 4), BF),
        pltpu.VMEM((XS, C, GROUP), BF),
        pltpu.VMEM((1, C, OA), BF),
        pltpu.VMEM((XS, C, GROUP), BF),
        pltpu.VMEM((XS, 32, QA + GROUP), BF),
        pltpu.VMEM((XS, 32, OA + GROUP), BF),
        pltpu.VMEM((4, 32, QA + GROUP), BF),
        pltpu.VMEM((4, 32, OA + GROUP), BF),
        pltpu.VMEM((ROWS, QA + GROUP), F32),
        pltpu.VMEM((2, 256, 3 * C), BF),
        pltpu.VMEM((2, 256, C), BF),
        pltpu.VMEM((2, 256, C), BF),
        pltpu.VMEM((2, 2, 128, C), BF),
        pltpu.VMEM((2, 128, C), BF),
        pltpu.VMEM((2, 128, C), BF),
        dma((2, 15)), dma((2, 15)), dma((2, 15)), dma((2, 15)),
        dma((2, 2)), dma((2, 2)), dma((2, 4)), dma((2, 4)),
    ]
    for count, across in ((4, False), (XS, True), (1, False), (XS, True)):
        scratch += Gather.sems(count, across)
    return pl.pallas_call(
        kernel,
        out_shape=jax.ShapeDtypeStruct(latents.shape, latents.dtype),
        in_specs=[vmem] * 5 + [pl.BlockSpec(memory_space=pltpu.SMEM)],
        out_specs=vmem,
        scratch_shapes=scratch,
        compiler_params=pltpu.CompilerParams(
            collective_id=0, has_side_effects=True, vmem_limit_bytes=56 * 1024 * 1024
        ),
        cost_estimate=pl.CostEstimate(
            flops=4 * 10**9, bytes_accessed=2 * 10**6, transcendentals=10**6
        ),
    )(latents, norm_gain, qkv_weight, out_weight, conv_weight, view_slope)


def solution(mesh):
    in_specs = (
        P("view", "frame", None, None),
        P(),
        P("frame", None),
        P("frame", None),
        P(None, "frame", None),
        P(),
    )
    return jax.shard_map(
        per_device,
        mesh=mesh,
        in_specs=in_specs,
        out_specs=P("view", "frame", None, None),
        check_vma=False,
    )
```

```python
import jax
import jax.numpy as jnp
from jax import lax
from jax.experimental import pallas as pl
from jax.experimental.pallas import tpu as pltpu
from jax.sharding import PartitionSpec as P

ZS, YLS, XS, YHS = 8, 2, 4, 4
VIEWS, PIX, C, HEADS = 16, 256, 640, 10
ROWS = 80
CUT = 48
QW, OW, SPLIT = 640, 512, 256
PEERS = [(dy, dz) for dz in (4, 3, 5, 2, 6, 1, 7, 0) for dy in (0, 1) if (dy, dz) != (0, 0)]
BF, F32 = jnp.bfloat16, jnp.float32


class Place:
    def __init__(self):
        v, f = lax.axis_index("view"), lax.axis_index("frame")
        self.view, self.frame = v, f
        self.yl, self.z = v // ZS, v % ZS
        self.yh, self.x, self.core = f // (XS * 2), (f // 2) % XS, f % 2
        self.even = self.yl == 0
        self.odd = self.yl == 1

    def at(self, yl, z, yh, x, core):
        return (yl * ZS + z, yh * (XS * 2) + x * 2 + core)

    def x_peer(self, d):
        return (self.view, self.yh * (XS * 2) + ((self.x + d + XS) % XS) * 2 + self.core)

    def y_peer(self, d):
        y = (self.yh * 2 + self.yl + d + 8) % 8
        return self.at(y % 2, self.z, y // 2, self.x, self.core)

    def sibling(self):
        return (self.view, self.yh * (XS * 2) + self.x * 2 + 1 - self.core)

    def frame_peer(self, d):
        return (self.view, (self.frame + d + 32) % 32)

    def view_peer(self, dy, dz):
        view = ((self.yl + dy) % YLS) * ZS + (self.z + dz) % ZS
        return view, (view, self.frame)


def remote(src, dst, send, recv, device):
    return pltpu.make_async_remote_copy(
        src_ref=src, dst_ref=dst, send_sem=send, recv_sem=recv,
        device_id=device, device_id_type=pl.DeviceIdType.MESH,
    )


class Gather:
    def __init__(self, here, buf, across, sems):
        self.h, self.buf, self.across = here, buf, across
        self.side = 2 * here.yl - 1
        (self.ys, self.yr, self.xs, self.xr, self.ss, self.sr) = sems

    def piece(self, b, p, part):
        start, rows = part
        row = pl.multiple_of((((b + 8) % YHS) * 2 + self.h.core) * ROWS + start, 16)
        return self.buf.at[p, pl.ds(row, rows)]

    def copy(self, b, p, send, recv, device, part=(0, ROWS)):
        ref = self.piece(b, p, part)
        return remote(ref, ref, send, recv, device)

    def hop(self, k, i, b, p):
        d = (self.side, -self.side, self.side)[k]
        return self.copy(b, p, self.ys.at[k, i], self.yr.at[k, i], self.h.y_peer(d))

    def to_sibling(self, b, p):
        i = ((b + 8) % YHS) * XS + p
        self.copy(b, p, self.ss.at[i], self.sr.at[i], self.h.sibling()).start()

    def pass_on(self, k, b, p):
        if self.across:
            for i in range(2):
                self.turn(i, k, b, 0).start()
        self.to_sibling(b, p)

    def turn(self, i, k, b, rel):
        part = ((0, ROWS), (0, ROWS), (0, CUT), (CUT, ROWS - CUT))[i]
        device = self.h.x_peer((1, -1)[i % 2])
        p = (self.h.x + rel) % XS
        return self.copy(b, p, self.xs.at[i, k], self.xr.at[i, k], device, part)

    def near(self, k, b):
        for i, rel in enumerate((3, 1)):
            self.turn(i, k, b, rel).wait_recv()
            self.turn(2 + i, k, b, rel).start()
            self.to_sibling(b, (self.h.x + rel) % XS)

    def far(self, k, b):
        for i in range(2, 4):
            self.turn(i, k, b, 2).wait_recv()
        self.to_sibling(b, (self.h.x + 2) % XS)

    def direct(self, i, rel):
        device = self.h.x_peer((1, -1, 2)[i])
        p = (self.h.x + rel) % XS
        return self.copy(self.h.yh, p, self.xs.at[i, 0], self.xr.at[i, 0], device)

    def steps(self):
        h = self.h
        own = [h.x] if self.across else [(h.x + rel) % XS for rel in (0, 3, 1, 2)]
        blocks = (h.yh + self.side, h.yh - self.side, h.yh + 2)
        self.hop(0, 0, h.yh, h.x).start()
        if not self.across:
            for i in range(3):
                self.direct(i, 0).start()
        self.pass_on(0, h.yh, h.x)
        yield
        if not self.across:
            for i, rel in enumerate((3, 1, 2)):
                self.direct(i, rel).wait_recv()
                self.hop(0, i + 1, h.yh, own[i + 1]).start()
                self.to_sibling(h.yh, own[i + 1])
            yield
        for k in range(3):
            for i, p in enumerate(own):
                self.hop(k, i, blocks[k], p).wait_recv()
                if k < 2:
                    self.hop(k + 1, i, blocks[k], p).start()
                self.pass_on(k + 1, blocks[k], p)
            if self.across:
                self.near(k, ((h.yh,) + blocks)[k])
            yield
        if self.across:
            self.near(3, blocks[2])
            yield
            for k, b in enumerate((h.yh,) + blocks):
                self.far(k, b)
            yield

    def arrive(self):
        for i in range(YHS * XS):
            self.copy(0, 0, self.ss.at[i], self.sr.at[i], self.h.sibling()).wait_recv()

    def drain(self):
        own = 1 if self.across else XS
        waits = [self.ys.at[k, i] for k in range(3) for i in range(own)]
        waits += [self.ss.at[i] for i in range(YHS * XS)]
        for sem in waits:
            self.copy(0, 0, sem, self.sr.at[0], self.h.sibling()).wait_send()
        if self.across:
            for i in range(4):
                for k in range(4):
                    self.turn(i, k, 0, 0).wait_send()
        else:
            for i in range(3):
                self.direct(i, 0).wait_send()

    @staticmethod
    def sems():
        shapes = ((3, 4), (3, 4), (4, 4), (4, 4), (16,), (16,))
        return [pltpu.SemaphoreType.DMA(k) for k in shapes]


def advance(*generators, times=1):
    for _ in range(times):
        for g in generators:
            next(g, None)


def kernel(
    lat, gain, qsh, osh, csh, slope, out,
    pieces, xin, outb, back, dist, wqa, wqb, woa, wob, sq, so, r1q, r1o, r32, qkv, mix, hid,
    hsend, hleft, hright,
    in_s, in_r, out_s, out_r, halo_s, halo_r, s1_s, s1_r, *sems,
):
    h = Place()
    barrier = pltpu.get_barrier_semaphore()
    partners = [h.view_peer(*p)[1] for p in PEERS]
    for dx in range(XS):
        for dc in range(2):
            if dx or dc:
                partners.append(
                    (h.view, h.yh * 8 + ((h.x + dx) % XS) * 2 + (h.core + dc) % 2)
                )
    partners += [h.y_peer(1), h.y_peer(-1), h.frame_peer(1), h.frame_peer(-1)]
    for p in partners:
        pl.semaphore_signal(barrier, inc=1, device_id=p, device_id_type=pl.DeviceIdType.MESH)

    for x in range(XS):
        sq[x, 0:20] = qsh[:, QW * x : QW * (x + 1)] if x < 3 else osh[...]
        sq[x, 20:32] = jnp.zeros((12, QW), BF)
        at, end = OW * x, min(OW * (x + 1), 3 * C)
        while at < end:
            t = at // C
            stop = min(end, C * (t + 1))
            so[x, 0:20, at - OW * x : stop - OW * x] = csh[t, :, at - C * t : stop - C * t]
            at = stop
        if end < OW * (x + 1):
            so[x, 0:20, end - OW * x :] = jnp.zeros((20, OW * (x + 1) - end), BF)
        so[x, 20:32] = jnp.zeros((12, OW), BF)
    both = [lat[0, f].astype(F32).reshape(32, 8, C) for f in range(2)]
    pieces[...] = jnp.stack(both, axis=1).reshape(32, 16, C).astype(BF)
    row = lax.broadcasted_iota(jnp.int32, (256, 256), 0)
    col = lax.broadcasted_iota(jnp.int32, (256, 256), 1)
    gap = jnp.abs(row // 16 - col // 16)
    gap = jnp.minimum(gap, VIEWS - gap).astype(F32)
    dist[...] = jnp.where(row % 16 == col % 16, gap, 1e30)

    pl.semaphore_wait(barrier, len(partners))

    half = h.x // 2
    slot = (h.x % 2) * 2 + h.core
    stages = ((sq, r1q, QW), (so, r1o, OW))

    def shard(t, x):
        src, dst = stages[t][:2]
        device = (h.view, h.yh * 8 + x * 2 + half)
        return remote(
            src.at[x], dst.at[slot], s1_s.at[t, x], s1_r.at[t, slot], device
        )

    mine = half == h.core
    for t in range(2):
        for x in range(XS):
            src, dst = stages[t][:2]

            @pl.when(jnp.logical_not(mine & (h.x == x)))
            def _():
                shard(t, x).start()

            @pl.when(mine & (h.x == x))
            def _():
                pltpu.make_async_copy(src.at[x], dst.at[slot], s1_r.at[t, slot]).start()

    def send_in(c, i):
        v, device = h.view_peer(*PEERS[i])
        return remote(
            pieces.at[v * 2 + c], xin.at[c, h.view], in_s.at[c, i], in_r.at[c, i], device
        )

    for c in range(2):
        for i in range(15):
            send_in(c, i).start()
        xin[c, h.view] = pieces[h.view * 2 + c]

    def put_together(t):
        dst, width = stages[t][1:]
        for s in range(4):
            pltpu.make_async_copy(dst.at[s], dst.at[s], s1_r.at[t, s]).wait()
            r32[20 * s : 20 * s + 20, 0:width] = dst[s, 0:20, :].astype(F32)
        rows = pl.ds(pl.multiple_of((h.yh * 2 + h.core) * ROWS, 16), ROWS)
        a, b = ((wqa, wqb), (woa, wob))[t]
        a[h.x, rows] = r32[:, 0:SPLIT].astype(BF)
        b[h.x, rows] = r32[:, SPLIT:width].astype(BF)

    qa = Gather(h, wqa, False, sems[0:6])
    qb = Gather(h, wqb, True, sems[6:12])
    oa = Gather(h, woa, False, sems[12:18])
    ob = Gather(h, wob, True, sems[18:24])
    sqa, sqb, soa, sob = qa.steps(), qb.steps(), oa.steps(), ob.steps()

    put_together(0)
    advance(sqb, sqa)
    put_together(1)
    advance(sob, soa)
    advance(sqa, sqb)
    advance(sqa, sqb)
    advance(soa, sob)
    advance(sqa, sqb)
    advance(soa, sob)
    advance(sqa, sqb)
    advance(soa, sob)
    advance(sqb)
    qa.arrive()
    qb.arrive()

    def project(c):
        for i in range(15):
            send_in(c, i).wait_recv()
        wide = xin[c].reshape(256, C).astype(F32)
        scale = lax.rsqrt(jnp.mean(wide * wide, axis=-1, keepdims=True) + 1e-06)
        normed = (wide * scale * gain[...].reshape(1, C)).astype(BF)
        tiles = [(QW * p + at, w[p]) for p in range(3) for at, w in ((0, wqa), (SPLIT, wqb))]
        for at, w in tiles:
            qkv[c, :, at : at + w.shape[1]] = jnp.dot(
                normed, w, preferred_element_type=F32
            ).astype(BF)

    low = lax.broadcasted_iota(jnp.int32, (256, 128), 1) < 64

    def attend(c, s):
        q = qkv[c, :, 128 * s : 128 * (s + 1)]
        k = qkv[c, :, 640 + 128 * s : 640 + 128 * (s + 1)]
        v = qkv[c, :, 1280 + 128 * s : 1280 + 128 * (s + 1)]
        v = jnp.concatenate([v, jnp.ones_like(v)], axis=1)
        parts = []
        for e in range(2):
            qe = jnp.where(low if e == 0 else jnp.logical_not(low), q, jnp.zeros_like(q))
            scores = lax.dot_general(
                qe, k, (((1,), (1,)), ((), ())), preferred_element_type=F32
            )
            scores = scores * 0.125 - slope[2 * s + e] * dist[...]
            top = jnp.max(scores, axis=-1, keepdims=True)
            weights = jnp.exp(scores - top).astype(BF)
            o = jnp.dot(weights, v, preferred_element_type=F32)
            parts.append(o[:, 0:128] / o[:, 128:256])
        mix[c, :, 128 * s : 128 * (s + 1)] = jnp.where(low, parts[0], parts[1]).astype(BF)

    def halo(c, side):
        dst = (hright, hleft)[side]
        return remote(
            hsend.at[c, side], dst.at[c], halo_s.at[c, side], halo_r.at[c, side],
            h.frame_peer((-1, 1)[side]),
        )

    taps_of = (
        lambda: (woa[0], wob[0], woa[1, :, 0:128]),
        lambda: (woa[1, :, 128:256], wob[1], woa[2]),
        lambda: (wob[2], woa[3], wob[3, :, 0:128]),
        lambda: (wqa[3], wqb[3]),
    )

    def times(a, t):
        return jnp.concatenate(
            [jnp.dot(a, w, preferred_element_type=F32) for w in taps_of[t]()], axis=1
        )

    def add(c):
        wide = xin[c].reshape(256, C).astype(F32)
        hidden = (wide + times(mix[c], 3)).astype(BF)
        hid[c] = hidden
        split = hidden.astype(F32).reshape(16, 2, 8, C)
        for side in range(2):
            hsend[c, side] = split[:, side].reshape(128, C).astype(BF)
            halo(c, side).start()

    def convolve(c):
        for side in range(2):
            halo(c, side).wait_recv()
        wide = hid[c].astype(F32)
        split = wide.reshape(16, 2, 8, C)
        before = hleft[c].astype(F32).reshape(16, 8, C)
        after = hright[c].astype(F32).reshape(16, 8, C)
        before = jnp.where(h.frame == 0, 0.0, before)
        after = jnp.where(h.frame == 31, 0.0, after)
        taps = (
            jnp.stack([before, split[:, 0]], axis=1).reshape(256, C).astype(BF),
            hid[c],
            jnp.stack([split[:, 1], after], axis=1).reshape(256, C).astype(BF),
        )
        for t in range(3):
            wide = wide + times(taps[t], t)
        outb[c] = wide.astype(BF).reshape(16, 16, C)
        for i in range(15):
            send_out(c, i).start()
        back[c, h.view] = outb[c, h.view]

    def send_out(c, i):
        v, device = h.view_peer(*PEERS[i])
        return remote(
            outb.at[c, v], back.at[c, h.view], out_s.at[c, i], out_r.at[c, i], device
        )

    project(0)
    advance(soa, sob)
    for k in range(5):
        attend(0, k)
    add(0)
    advance(sob)
    project(1)
    for k in range(5):
        attend(1, k)
    add(1)
    oa.arrive()
    ob.arrive()
    convolve(0)
    convolve(1)

    for g in (qa, qb, oa, ob):
        g.drain()
    for t in range(2):
        for x in range(XS):
            @pl.when(jnp.logical_not(mine & (h.x == x)))
            def _():
                shard(t, x).wait_send()
    for c in range(2):
        for side in range(2):
            halo(c, side).wait_send()
        for i in range(15):
            send_in(c, i).wait_send()
    for c in range(2):
        for i in range(15):
            send_out(c, i).wait_recv()
    both = [back[c].astype(F32).reshape(16, 2, 8, C) for c in range(2)]
    for f in range(2):
        out[0, f] = jnp.stack([b[:, f] for b in both], axis=1).reshape(PIX, C).astype(BF)
    for c in range(2):
        for i in range(15):
            send_out(c, i).wait_send()


def per_device(latents, norm_gain, qkv_weight, out_weight, conv_weight, view_slope):
    vmem = pl.BlockSpec(memory_space=pltpu.VMEM)
    dma = pltpu.SemaphoreType.DMA
    scratch = [
        pltpu.VMEM((32, 16, C), BF),
        pltpu.VMEM((2, 16, 16, C), BF),
        pltpu.VMEM((2, 16, 16, C), BF),
        pltpu.VMEM((2, 16, 16, C), BF),
        pltpu.VMEM((256, 256), F32),
        pltpu.VMEM((XS, C, SPLIT), BF),
        pltpu.VMEM((XS, C, QW - SPLIT), BF),
        pltpu.VMEM((XS, C, SPLIT), BF),
        pltpu.VMEM((XS, C, OW - SPLIT), BF),
        pltpu.VMEM((XS, 32, QW), BF),
        pltpu.VMEM((XS, 32, OW), BF),
        pltpu.VMEM((4, 32, QW), BF),
        pltpu.VMEM((4, 32, OW), BF),
        pltpu.VMEM((ROWS, QW), F32),
        pltpu.VMEM((2, 256, 3 * C), BF),
        pltpu.VMEM((2, 256, C), BF),
        pltpu.VMEM((2, 256, C), BF),
        pltpu.VMEM((2, 2, 128, C), BF),
        pltpu.VMEM((2, 128, C), BF),
        pltpu.VMEM((2, 128, C), BF),
        dma((2, 15)), dma((2, 15)), dma((2, 15)), dma((2, 15)),
        dma((2, 2)), dma((2, 2)), dma((2, 4)), dma((2, 4)),
    ]
    for _ in range(4):
        scratch += Gather.sems()
    return pl.pallas_call(
        kernel,
        out_shape=jax.ShapeDtypeStruct(latents.shape, latents.dtype),
        in_specs=[vmem] * 5 + [pl.BlockSpec(memory_space=pltpu.SMEM)],
        out_specs=vmem,
        scratch_shapes=scratch,
        compiler_params=pltpu.CompilerParams(
            collective_id=0, has_side_effects=True, vmem_limit_bytes=56 * 1024 * 1024
        ),
        cost_estimate=pl.CostEstimate(
            flops=4 * 10**9, bytes_accessed=2 * 10**6, transcendentals=10**6
        ),
    )(latents, norm_gain, qkv_weight, out_weight, conv_weight, view_slope)


def solution(mesh):
    in_specs = (
        P("view", "frame", None, None),
        P(),
        P("frame", None),
        P("frame", None),
        P(None, "frame", None),
        P(),
    )
    return jax.shard_map(
        per_device,
        mesh=mesh,
        in_specs=in_specs,
        out_specs=P("view", "frame", None, None),
        check_vma=False,
    )
```

```python
import jax
import jax.numpy as jnp
from jax import lax
from jax.experimental import pallas as pl
from jax.experimental.pallas import tpu as pltpu
from jax.sharding import PartitionSpec as P

ZS, YLS, XS, YHS = 8, 2, 4, 4
VIEWS, PIX, C, HEADS = 16, 256, 640, 10
ROWS = 80
CUT = 48
QW, OW, SPLIT = 640, 512, 256
PEERS = [(dy, dz) for dz in (4, 3, 5, 2, 6, 1, 7, 0) for dy in (0, 1) if (dy, dz) != (0, 0)]
BF, F32 = jnp.bfloat16, jnp.float32


class Place:
    def __init__(self):
        v, f = lax.axis_index("view"), lax.axis_index("frame")
        self.view, self.frame = v, f
        self.yl, self.z = v // ZS, v % ZS
        self.yh, self.x, self.core = f // (XS * 2), (f // 2) % XS, f % 2
        self.even = self.yl == 0
        self.odd = self.yl == 1

    def at(self, yl, z, yh, x, core):
        return (yl * ZS + z, yh * (XS * 2) + x * 2 + core)

    def x_peer(self, d):
        return (self.view, self.yh * (XS * 2) + ((self.x + d + XS) % XS) * 2 + self.core)

    def y_peer(self, d):
        y = (self.yh * 2 + self.yl + d + 8) % 8
        return self.at(y % 2, self.z, y // 2, self.x, self.core)

    def sibling(self):
        return (self.view, self.yh * (XS * 2) + self.x * 2 + 1 - self.core)

    def frame_peer(self, d):
        return (self.view, (self.frame + d + 32) % 32)

    def view_peer(self, dy, dz):
        view = ((self.yl + dy) % YLS) * ZS + (self.z + dz) % ZS
        return view, (view, self.frame)


def remote(src, dst, send, recv, device):
    return pltpu.make_async_remote_copy(
        src_ref=src, dst_ref=dst, send_sem=send, recv_sem=recv,
        device_id=device, device_id_type=pl.DeviceIdType.MESH,
    )


class Gather:
    def __init__(self, here, buf, across, sems):
        self.h, self.buf, self.across = here, buf, across
        self.side = 2 * here.yl - 1
        (self.ys, self.yr, self.xs, self.xr, self.ss, self.sr) = sems

    def piece(self, b, p, part):
        start, rows = part
        row = pl.multiple_of((((b + 8) % YHS) * 2 + self.h.core) * ROWS + start, 16)
        return self.buf.at[p, pl.ds(row, rows)]

    def copy(self, b, p, send, recv, device, part=(0, ROWS)):
        ref = self.piece(b, p, part)
        return remote(ref, ref, send, recv, device)

    def hop(self, k, i, b, p):
        d = (self.side, -self.side, self.side)[k]
        return self.copy(b, p, self.ys.at[k, i], self.yr.at[k, i], self.h.y_peer(d))

    def to_sibling(self, b, p):
        i = ((b + 8) % YHS) * XS + p
        self.copy(b, p, self.ss.at[i], self.sr.at[i], self.h.sibling()).start()

    def pass_on(self, k, b, p):
        if self.across:
            for i in range(3 if k == 3 else 2):
                self.turn(i, k, b, 0).start()
        self.to_sibling(b, p)

    def turn(self, i, k, b, rel):
        part = ((0, ROWS), (0, ROWS), (0, CUT), (CUT, ROWS - CUT))[i]
        device = self.h.x_peer((1, -1)[i % 2])
        if i == 2 and k == 3:
            part, device = (0, ROWS), self.h.x_peer(2)
        p = (self.h.x + rel) % XS
        return self.copy(b, p, self.xs.at[i, k], self.xr.at[i, k], device, part)

    def near(self, k, b):
        for i, rel in enumerate((3, 1)):
            self.turn(i, k, b, rel).wait_recv()
            if k < 3:
                self.turn(2 + i, k, b, rel).start()
            self.to_sibling(b, (self.h.x + rel) % XS)

    def far(self, k, b):
        for i in range(2, 3 if k == 3 else 4):
            self.turn(i, k, b, 2).wait_recv()
        self.to_sibling(b, (self.h.x + 2) % XS)

    def direct(self, i, rel):
        device = self.h.x_peer((1, -1, 2)[i])
        p = (self.h.x + rel) % XS
        return self.copy(self.h.yh, p, self.xs.at[i, 0], self.xr.at[i, 0], device)

    def steps(self):
        h = self.h
        own = [h.x] if self.across else [(h.x + rel) % XS for rel in (0, 3, 1, 2)]
        blocks = (h.yh + self.side, h.yh - self.side, h.yh + 2)
        self.hop(0, 0, h.yh, h.x).start()
        if not self.across:
            for i in range(3):
                self.direct(i, 0).start()
        self.pass_on(0, h.yh, h.x)
        yield
        if not self.across:
            for i, rel in enumerate((3, 1, 2)):
                self.direct(i, rel).wait_recv()
                self.hop(0, i + 1, h.yh, own[i + 1]).start()
                self.to_sibling(h.yh, own[i + 1])
            yield
        for k in range(3):
            for i, p in enumerate(own):
                self.hop(k, i, blocks[k], p).wait_recv()
                if k < 2:
                    self.hop(k + 1, i, blocks[k], p).start()
                self.pass_on(k + 1, blocks[k], p)
            if self.across:
                self.near(k, ((h.yh,) + blocks)[k])
            yield
        if self.across:
            self.near(3, blocks[2])
            yield
            for k, b in enumerate((h.yh,) + blocks):
                self.far(k, b)
            yield

    def arrive(self):
        for i in range(YHS * XS):
            self.copy(0, 0, self.ss.at[i], self.sr.at[i], self.h.sibling()).wait_recv()

    def drain(self):
        own = 1 if self.across else XS
        waits = [self.ys.at[k, i] for k in range(3) for i in range(own)]
        waits += [self.ss.at[i] for i in range(YHS * XS)]
        for sem in waits:
            self.copy(0, 0, sem, self.sr.at[0], self.h.sibling()).wait_send()
        if self.across:
            for i in range(4):
                for k in range(3 if i == 3 else 4):
                    self.turn(i, k, 0, 0).wait_send()
        else:
            for i in range(3):
                self.direct(i, 0).wait_send()

    @staticmethod
    def sems():
        shapes = ((3, 4), (3, 4), (4, 4), (4, 4), (16,), (16,))
        return [pltpu.SemaphoreType.DMA(k) for k in shapes]


def advance(*generators, times=1):
    for _ in range(times):
        for g in generators:
            next(g, None)


def kernel(
    lat, gain, qsh, osh, csh, slope, out,
    pieces, xin, outb, back, dist, wqa, wqb, woa, wob, sq, so, r1q, r1o, r32, qkv, mix, hid,
    hsend, hleft, hright,
    in_s, in_r, out_s, out_r, halo_s, halo_r, s1_s, s1_r, *sems,
):
    h = Place()
    barrier = pltpu.get_barrier_semaphore()
    partners = [h.view_peer(*p)[1] for p in PEERS]
    for dx in range(XS):
        for dc in range(2):
            if dx or dc:
                partners.append(
                    (h.view, h.yh * 8 + ((h.x + dx) % XS) * 2 + (h.core + dc) % 2)
                )
    partners += [h.y_peer(d) for d in (1, -1)]
    partners += [h.frame_peer(1), h.frame_peer(-1)]
    for p in partners:
        pl.semaphore_signal(barrier, inc=1, device_id=p, device_id_type=pl.DeviceIdType.MESH)

    for x in range(XS):
        sq[x, 0:20] = qsh[:, QW * x : QW * (x + 1)] if x < 3 else osh[...]
        sq[x, 20:32] = jnp.zeros((12, QW), BF)
        at, end = OW * x, min(OW * (x + 1), 3 * C)
        while at < end:
            t = at // C
            stop = min(end, C * (t + 1))
            so[x, 0:20, at - OW * x : stop - OW * x] = csh[t, :, at - C * t : stop - C * t]
            at = stop
        if end < OW * (x + 1):
            so[x, 0:20, end - OW * x :] = jnp.zeros((20, OW * (x + 1) - end), BF)
        so[x, 20:32] = jnp.zeros((12, OW), BF)
    both = [lat[0, f].astype(F32).reshape(32, 8, C) for f in range(2)]
    pieces[...] = jnp.stack(both, axis=1).reshape(32, 16, C).astype(BF)
    row = lax.broadcasted_iota(jnp.int32, (256, 256), 0)
    col = lax.broadcasted_iota(jnp.int32, (256, 256), 1)
    gap = jnp.abs(row // 16 - col // 16)
    gap = jnp.minimum(gap, VIEWS - gap).astype(F32)
    dist[...] = jnp.where(row % 16 == col % 16, gap, 1e30)

    pl.semaphore_wait(barrier, len(partners))

    half = h.x // 2
    slot = (h.x % 2) * 2 + h.core
    stages = ((sq, r1q, QW), (so, r1o, OW))

    def shard(t, x):
        src, dst = stages[t][:2]
        device = (h.view, h.yh * 8 + x * 2 + half)
        return remote(
            src.at[x], dst.at[slot], s1_s.at[t, x], s1_r.at[t, slot], device
        )

    mine = half == h.core
    for t in range(2):
        for x in range(XS):
            src, dst = stages[t][:2]

            @pl.when(jnp.logical_not(mine & (h.x == x)))
            def _():
                shard(t, x).start()

            @pl.when(mine & (h.x == x))
            def _():
                pltpu.make_async_copy(src.at[x], dst.at[slot], s1_r.at[t, slot]).start()

    def send_in(c, i):
        v, device = h.view_peer(*PEERS[i])
        return remote(
            pieces.at[v * 2 + c], xin.at[c, h.view], in_s.at[c, i], in_r.at[c, i], device
        )

    for c in range(2):
        for i in range(15):
            send_in(c, i).start()
        xin[c, h.view] = pieces[h.view * 2 + c]

    def put_together(t):
        dst, width = stages[t][1:]
        for s in range(4):
            pltpu.make_async_copy(dst.at[s], dst.at[s], s1_r.at[t, s]).wait()
            r32[20 * s : 20 * s + 20, 0:width] = dst[s, 0:20, :].astype(F32)
        rows = pl.ds(pl.multiple_of((h.yh * 2 + h.core) * ROWS, 16), ROWS)
        a, b = ((wqa, wqb), (woa, wob))[t]
        a[h.x, rows] = r32[:, 0:SPLIT].astype(BF)
        b[h.x, rows] = r32[:, SPLIT:width].astype(BF)

    qa = Gather(h, wqa, False, sems[0:6])
    qb = Gather(h, wqb, True, sems[6:12])
    oa = Gather(h, woa, False, sems[12:18])
    ob = Gather(h, wob, True, sems[18:24])
    sqa, sqb, soa, sob = qa.steps(), qb.steps(), oa.steps(), ob.steps()

    put_together(0)
    advance(sqb, sqa)
    put_together(1)
    advance(sob, soa)
    advance(sqa, sqb)
    advance(sqa, sqb)
    advance(soa, sob)
    advance(sqa, sqb)
    advance(soa, sob)
    advance(sqa, sqb)
    advance(soa, sob)
    advance(sqb)
    qa.arrive()
    qb.arrive()

    def project(c):
        for i in range(15):
            send_in(c, i).wait_recv()
        wide = xin[c].reshape(256, C).astype(F32)
        scale = lax.rsqrt(jnp.mean(wide * wide, axis=-1, keepdims=True) + 1e-06)
        normed = (wide * scale * gain[...].reshape(1, C)).astype(BF)
        tiles = [(QW * p + at, w[p]) for p in range(3) for at, w in ((0, wqa), (SPLIT, wqb))]
        for at, w in tiles:
            qkv[c, :, at : at + w.shape[1]] = jnp.dot(
                normed, w, preferred_element_type=F32
            ).astype(BF)

    low = lax.broadcasted_iota(jnp.int32, (256, 128), 1) < 64

    def attend(c, s):
        q = qkv[c, :, 128 * s : 128 * (s + 1)]
        k = qkv[c, :, 640 + 128 * s : 640 + 128 * (s + 1)]
        v = qkv[c, :, 1280 + 128 * s : 1280 + 128 * (s + 1)]
        v = jnp.concatenate([v, jnp.ones_like(v)], axis=1)
        parts = []
        for e in range(2):
            qe = jnp.where(low if e == 0 else jnp.logical_not(low), q, jnp.zeros_like(q))
            scores = lax.dot_general(
                qe, k, (((1,), (1,)), ((), ())), preferred_element_type=F32
            )
            scores = scores * 0.125 - slope[2 * s + e] * dist[...]
            top = jnp.max(scores, axis=-1, keepdims=True)
            weights = jnp.exp(scores - top).astype(BF)
            o = jnp.dot(weights, v, preferred_element_type=F32)
            parts.append(o[:, 0:128] / o[:, 128:256])
        mix[c, :, 128 * s : 128 * (s + 1)] = jnp.where(low, parts[0], parts[1]).astype(BF)

    def halo(c, side):
        dst = (hright, hleft)[side]
        return remote(
            hsend.at[c, side], dst.at[c], halo_s.at[c, side], halo_r.at[c, side],
            h.frame_peer((-1, 1)[side]),
        )

    taps_of = (
        lambda: (woa[0], wob[0], woa[1, :, 0:128]),
        lambda: (woa[1, :, 128:256], wob[1], woa[2]),
        lambda: (wob[2], woa[3], wob[3, :, 0:128]),
        lambda: (wqa[3], wqb[3]),
    )

    def times(a, t):
        return jnp.concatenate(
            [jnp.dot(a, w, preferred_element_type=F32) for w in taps_of[t]()], axis=1
        )

    def add(c):
        wide = xin[c].reshape(256, C).astype(F32)
        hidden = (wide + times(mix[c], 3)).astype(BF)
        hid[c] = hidden
        split = hidden.astype(F32).reshape(16, 2, 8, C)
        for side in range(2):
            hsend[c, side] = split[:, side].reshape(128, C).astype(BF)
            halo(c, side).start()

    def convolve(c):
        for side in range(2):
            halo(c, side).wait_recv()
        wide = hid[c].astype(F32)
        split = wide.reshape(16, 2, 8, C)
        before = hleft[c].astype(F32).reshape(16, 8, C)
        after = hright[c].astype(F32).reshape(16, 8, C)
        before = jnp.where(h.frame == 0, 0.0, before)
        after = jnp.where(h.frame == 31, 0.0, after)
        taps = (
            jnp.stack([before, split[:, 0]], axis=1).reshape(256, C).astype(BF),
            hid[c],
            jnp.stack([split[:, 1], after], axis=1).reshape(256, C).astype(BF),
        )
        for t in range(3):
            wide = wide + times(taps[t], t)
        outb[c] = wide.astype(BF).reshape(16, 16, C)
        for i in range(15):
            send_out(c, i).start()
        back[c, h.view] = outb[c, h.view]

    def send_out(c, i):
        v, device = h.view_peer(*PEERS[i])
        return remote(
            outb.at[c, v], back.at[c, h.view], out_s.at[c, i], out_r.at[c, i], device
        )

    project(0)
    advance(soa, sob)
    for k in range(5):
        attend(0, k)
    add(0)
    advance(sob)
    project(1)
    for k in range(5):
        attend(1, k)
    add(1)
    oa.arrive()
    ob.arrive()
    convolve(0)
    convolve(1)

    for g in (qa, qb, oa, ob):
        g.drain()
    for t in range(2):
        for x in range(XS):
            @pl.when(jnp.logical_not(mine & (h.x == x)))
            def _():
                shard(t, x).wait_send()
    for c in range(2):
        for side in range(2):
            halo(c, side).wait_send()
        for i in range(15):
            send_in(c, i).wait_send()
    for c in range(2):
        for i in range(15):
            send_out(c, i).wait_recv()
    both = [back[c].astype(F32).reshape(16, 2, 8, C) for c in range(2)]
    for f in range(2):
        out[0, f] = jnp.stack([b[:, f] for b in both], axis=1).reshape(PIX, C).astype(BF)
    for c in range(2):
        for i in range(15):
            send_out(c, i).wait_send()


def per_device(latents, norm_gain, qkv_weight, out_weight, conv_weight, view_slope):
    vmem = pl.BlockSpec(memory_space=pltpu.VMEM)
    dma = pltpu.SemaphoreType.DMA
    scratch = [
        pltpu.VMEM((32, 16, C), BF),
        pltpu.VMEM((2, 16, 16, C), BF),
        pltpu.VMEM((2, 16, 16, C), BF),
        pltpu.VMEM((2, 16, 16, C), BF),
        pltpu.VMEM((256, 256), F32),
        pltpu.VMEM((XS, C, SPLIT), BF),
        pltpu.VMEM((XS, C, QW - SPLIT), BF),
        pltpu.VMEM((XS, C, SPLIT), BF),
        pltpu.VMEM((XS, C, OW - SPLIT), BF),
        pltpu.VMEM((XS, 32, QW), BF),
        pltpu.VMEM((XS, 32, OW), BF),
        pltpu.VMEM((4, 32, QW), BF),
        pltpu.VMEM((4, 32, OW), BF),
        pltpu.VMEM((ROWS, QW), F32),
        pltpu.VMEM((2, 256, 3 * C), BF),
        pltpu.VMEM((2, 256, C), BF),
        pltpu.VMEM((2, 256, C), BF),
        pltpu.VMEM((2, 2, 128, C), BF),
        pltpu.VMEM((2, 128, C), BF),
        pltpu.VMEM((2, 128, C), BF),
        dma((2, 15)), dma((2, 15)), dma((2, 15)), dma((2, 15)),
        dma((2, 2)), dma((2, 2)), dma((2, 4)), dma((2, 4)),
    ]
    for _ in range(4):
        scratch += Gather.sems()
    return pl.pallas_call(
        kernel,
        out_shape=jax.ShapeDtypeStruct(latents.shape, latents.dtype),
        in_specs=[vmem] * 5 + [pl.BlockSpec(memory_space=pltpu.SMEM)],
        out_specs=vmem,
        scratch_shapes=scratch,
        compiler_params=pltpu.CompilerParams(
            collective_id=0, has_side_effects=True, vmem_limit_bytes=56 * 1024 * 1024
        ),
        cost_estimate=pl.CostEstimate(
            flops=4 * 10**9, bytes_accessed=2 * 10**6, transcendentals=10**6
        ),
    )(latents, norm_gain, qkv_weight, out_weight, conv_weight, view_slope)


def solution(mesh):
    in_specs = (
        P("view", "frame", None, None),
        P(),
        P("frame", None),
        P("frame", None),
        P(None, "frame", None),
        P(),
    )
    return jax.shard_map(
        per_device,
        mesh=mesh,
        in_specs=in_specs,
        out_specs=P("view", "frame", None, None),
        check_vma=False,
    )
```

```python
import jax
import jax.numpy as jnp
from jax import lax
from jax.experimental import pallas as pl
from jax.experimental.pallas import tpu as pltpu
from jax.sharding import PartitionSpec as P

ZS, YLS, XS, YHS = 8, 2, 4, 4
VIEWS, PIX, C, HEADS = 16, 256, 640, 10
ROWS = 80
CUT = 48
QW, OW, SPLIT = 640, 512, 256
PEERS = [(dy, dz) for dz in (4, 3, 5, 2, 6, 1, 7, 0) for dy in (0, 1) if (dy, dz) != (0, 0)]
BF, F32 = jnp.bfloat16, jnp.float32


class Place:
    def __init__(self):
        v, f = lax.axis_index("view"), lax.axis_index("frame")
        self.view, self.frame = v, f
        self.yl, self.z = v // ZS, v % ZS
        self.yh, self.x, self.core = f // (XS * 2), (f // 2) % XS, f % 2
        self.even = self.yl == 0
        self.odd = self.yl == 1

    def at(self, yl, z, yh, x, core):
        return (yl * ZS + z, yh * (XS * 2) + x * 2 + core)

    def x_peer(self, d):
        return (self.view, self.yh * (XS * 2) + ((self.x + d + XS) % XS) * 2 + self.core)

    def y_peer(self, d):
        y = (self.yh * 2 + self.yl + d + 8) % 8
        return self.at(y % 2, self.z, y // 2, self.x, self.core)

    def sibling(self):
        return (self.view, self.yh * (XS * 2) + self.x * 2 + 1 - self.core)

    def frame_peer(self, d):
        return (self.view, (self.frame + d + 32) % 32)

    def view_peer(self, dy, dz):
        view = ((self.yl + dy) % YLS) * ZS + (self.z + dz) % ZS
        return view, (view, self.frame)


def remote(src, dst, send, recv, device):
    return pltpu.make_async_remote_copy(
        src_ref=src, dst_ref=dst, send_sem=send, recv_sem=recv,
        device_id=device, device_id_type=pl.DeviceIdType.MESH,
    )


class Gather:
    def __init__(self, here, buf, across, sems):
        self.h, self.buf, self.across = here, buf, across
        self.side = 2 * here.yl - 1
        (self.ys, self.yr, self.xs, self.xr, self.ss, self.sr) = sems

    def piece(self, b, p, part):
        start, rows = part
        row = pl.multiple_of((((b + 8) % YHS) * 2 + self.h.core) * ROWS + start, 16)
        return self.buf.at[p, pl.ds(row, rows)]

    def copy(self, b, p, send, recv, device, part=(0, ROWS)):
        ref = self.piece(b, p, part)
        return remote(ref, ref, send, recv, device)

    def hop(self, k, i, b, p):
        d = (self.side, -self.side, self.side)[k]
        return self.copy(b, p, self.ys.at[k, i], self.yr.at[k, i], self.h.y_peer(d))

    def to_sibling(self, b, p):
        i = ((b + 8) % YHS) * XS + p
        self.copy(b, p, self.ss.at[i], self.sr.at[i], self.h.sibling()).start()

    def pass_on(self, k, b, p):
        if self.across:
            for i in range(3 if k == 3 else 2):
                self.turn(i, k, b, 0).start()
        self.to_sibling(b, p)

    def turn(self, i, k, b, rel):
        part = ((0, ROWS), (0, ROWS), (0, CUT), (CUT, ROWS - CUT))[i]
        device = self.h.x_peer((1, -1)[i % 2])
        if i == 2 and k == 3:
            part, device = (0, ROWS), self.h.x_peer(2)
        p = (self.h.x + rel) % XS
        return self.copy(b, p, self.xs.at[i, k], self.xr.at[i, k], device, part)

    def near(self, k, b):
        for i, rel in enumerate((3, 1)):
            self.turn(i, k, b, rel).wait_recv()
            if k < 3:
                self.turn(2 + i, k, b, rel).start()
            self.to_sibling(b, (self.h.x + rel) % XS)

    def far(self, k, b):
        for i in range(2, 3 if k == 3 else 4):
            self.turn(i, k, b, 2).wait_recv()
        self.to_sibling(b, (self.h.x + 2) % XS)

    def direct(self, i, rel):
        device = self.h.x_peer((1, -1, 2)[i])
        p = (self.h.x + rel) % XS
        return self.copy(self.h.yh, p, self.xs.at[i, 0], self.xr.at[i, 0], device)

    def steps(self):
        h = self.h
        own = [h.x] if self.across else [(h.x + rel) % XS for rel in (0, 3, 1, 2)]
        blocks = (h.yh + self.side, h.yh - self.side, h.yh + 2)
        self.hop(0, 0, h.yh, h.x).start()
        if not self.across:
            for i in range(3):
                self.direct(i, 0).start()
        self.pass_on(0, h.yh, h.x)
        yield
        if not self.across:
            for i, rel in enumerate((3, 1, 2)):
                self.direct(i, rel).wait_recv()
                self.hop(0, i + 1, h.yh, own[i + 1]).start()
                self.to_sibling(h.yh, own[i + 1])
            yield
        for k in range(3):
            for i, p in enumerate(own):
                self.hop(k, i, blocks[k], p).wait_recv()
                if k < 2:
                    self.hop(k + 1, i, blocks[k], p).start()
                self.pass_on(k + 1, blocks[k], p)
            if self.across:
                self.near(k, ((h.yh,) + blocks)[k])
            yield
        if self.across:
            self.near(3, blocks[2])
            yield
            for k, b in enumerate((h.yh,) + blocks):
                self.far(k, b)
            yield

    def arrive(self):
        for i in range(YHS * XS):
            self.copy(0, 0, self.ss.at[i], self.sr.at[i], self.h.sibling()).wait_recv()

    def drain(self):
        own = 1 if self.across else XS
        waits = [self.ys.at[k, i] for k in range(3) for i in range(own)]
        waits += [self.ss.at[i] for i in range(YHS * XS)]
        for sem in waits:
            self.copy(0, 0, sem, self.sr.at[0], self.h.sibling()).wait_send()
        if self.across:
            for i in range(4):
                for k in range(3 if i == 3 else 4):
                    self.turn(i, k, 0, 0).wait_send()
        else:
            for i in range(3):
                self.direct(i, 0).wait_send()

    @staticmethod
    def sems():
        shapes = ((3, 4), (3, 4), (4, 4), (4, 4), (16,), (16,))
        return [pltpu.SemaphoreType.DMA(k) for k in shapes]


def advance(*generators, times=1):
    for _ in range(times):
        for g in generators:
            next(g, None)


def kernel(
    lat, gain, qsh, osh, csh, slope, out,
    pieces, xin, outb, back, dist, wqa, wqb, woa, wob, sq, so, r1q, r1o, r32, qkv, mix, hid,
    hsend, hleft, hright,
    in_s, in_r, out_s, out_r, halo_s, halo_r, s1_s, s1_r, *sems,
):
    h = Place()
    barrier = pltpu.get_barrier_semaphore()
    partners = [h.view_peer(*p)[1] for p in PEERS]
    for dx in range(XS):
        for dc in range(2):
            if dx or dc:
                partners.append(
                    (h.view, h.yh * 8 + ((h.x + dx) % XS) * 2 + (h.core + dc) % 2)
                )
    partners += [h.y_peer(d) for d in (1, -1)]
    partners += [h.frame_peer(1), h.frame_peer(-1)]
    for p in partners:
        pl.semaphore_signal(barrier, inc=1, device_id=p, device_id_type=pl.DeviceIdType.MESH)

    for x in range(XS):
        sq[x, 0:20] = qsh[:, QW * x : QW * (x + 1)] if x < 3 else osh[...]
        sq[x, 20:32] = jnp.zeros((12, QW), BF)
        at, end = OW * x, min(OW * (x + 1), 3 * C)
        while at < end:
            t = at // C
            stop = min(end, C * (t + 1))
            so[x, 0:20, at - OW * x : stop - OW * x] = csh[t, :, at - C * t : stop - C * t]
            at = stop
        if end < OW * (x + 1):
            so[x, 0:20, end - OW * x :] = jnp.zeros((20, OW * (x + 1) - end), BF)
        so[x, 20:32] = jnp.zeros((12, OW), BF)
    both = [lat[0, f].astype(F32).reshape(32, 8, C) for f in range(2)]
    pieces[...] = jnp.stack(both, axis=1).reshape(32, 16, C).astype(BF)
    row = lax.broadcasted_iota(jnp.int32, (256, 256), 0)
    col = lax.broadcasted_iota(jnp.int32, (256, 256), 1)
    gap = jnp.abs(row // 16 - col // 16)
    gap = jnp.minimum(gap, VIEWS - gap).astype(F32)
    dist[...] = jnp.where(row % 16 == col % 16, gap, 1e30)

    pl.semaphore_wait(barrier, len(partners))

    half = h.x // 2
    slot = (h.x % 2) * 2 + h.core
    stages = ((sq, r1q, QW), (so, r1o, OW))

    def shard(t, x):
        src, dst = stages[t][:2]
        device = (h.view, h.yh * 8 + x * 2 + half)
        return remote(
            src.at[x], dst.at[slot], s1_s.at[t, x], s1_r.at[t, slot], device
        )

    mine = half == h.core
    for t in range(2):
        for x in range(XS):
            src, dst = stages[t][:2]

            @pl.when(jnp.logical_not(mine & (h.x == x)))
            def _():
                shard(t, x).start()

            @pl.when(mine & (h.x == x))
            def _():
                pltpu.make_async_copy(src.at[x], dst.at[slot], s1_r.at[t, slot]).start()

    def send_in(c, i):
        v, device = h.view_peer(*PEERS[i])
        return remote(
            pieces.at[v * 2 + c], xin.at[c, h.view], in_s.at[c, i], in_r.at[c, i], device
        )

    for c in range(2):
        for i in range(15):
            send_in(c, i).start()
        xin[c, h.view] = pieces[h.view * 2 + c]

    def put_together(t):
        dst, width = stages[t][1:]
        for s in range(4):
            pltpu.make_async_copy(dst.at[s], dst.at[s], s1_r.at[t, s]).wait()
            r32[20 * s : 20 * s + 20, 0:width] = dst[s, 0:20, :].astype(F32)
        rows = pl.ds(pl.multiple_of((h.yh * 2 + h.core) * ROWS, 16), ROWS)
        a, b = ((wqa, wqb), (woa, wob))[t]
        a[h.x, rows] = r32[:, 0:SPLIT].astype(BF)
        b[h.x, rows] = r32[:, SPLIT:width].astype(BF)

    qa = Gather(h, wqa, False, sems[0:6])
    qb = Gather(h, wqb, True, sems[6:12])
    oa = Gather(h, woa, False, sems[12:18])
    ob = Gather(h, wob, True, sems[18:24])
    sqa, sqb, soa, sob = qa.steps(), qb.steps(), oa.steps(), ob.steps()

    put_together(0)
    advance(sqb, sqa)
    put_together(1)
    advance(sqa, sqb)
    advance(sob, soa)
    advance(sqa, sqb)
    advance(soa, sob)
    advance(sqa, sqb)
    advance(soa, sob)
    advance(sqa, sqb)
    advance(soa, sob)
    advance(sqb)
    qa.arrive()
    qb.arrive()

    def project(c):
        for i in range(15):
            send_in(c, i).wait_recv()
        wide = xin[c].reshape(256, C).astype(F32)
        scale = lax.rsqrt(jnp.mean(wide * wide, axis=-1, keepdims=True) + 1e-06)
        normed = (wide * scale * gain[...].reshape(1, C)).astype(BF)
        tiles = [(QW * p + at, w[p]) for p in range(3) for at, w in ((0, wqa), (SPLIT, wqb))]
        for at, w in tiles:
            qkv[c, :, at : at + w.shape[1]] = jnp.dot(
                normed, w, preferred_element_type=F32
            ).astype(BF)

    low = lax.broadcasted_iota(jnp.int32, (256, 128), 1) < 64

    def attend(c, s):
        q = qkv[c, :, 128 * s : 128 * (s + 1)]
        k = qkv[c, :, 640 + 128 * s : 640 + 128 * (s + 1)]
        v = qkv[c, :, 1280 + 128 * s : 1280 + 128 * (s + 1)]
        v = jnp.concatenate([v, jnp.ones_like(v)], axis=1)
        parts = []
        for e in range(2):
            qe = jnp.where(low if e == 0 else jnp.logical_not(low), q, jnp.zeros_like(q))
            scores = lax.dot_general(
                qe, k, (((1,), (1,)), ((), ())), preferred_element_type=F32
            )
            scores = scores * 0.125 - slope[2 * s + e] * dist[...]
            top = jnp.max(scores, axis=-1, keepdims=True)
            weights = jnp.exp(scores - top).astype(BF)
            o = jnp.dot(weights, v, preferred_element_type=F32)
            parts.append(o[:, 0:128] / o[:, 128:256])
        mix[c, :, 128 * s : 128 * (s + 1)] = jnp.where(low, parts[0], parts[1]).astype(BF)

    def halo(c, side):
        dst = (hright, hleft)[side]
        return remote(
            hsend.at[c, side], dst.at[c], halo_s.at[c, side], halo_r.at[c, side],
            h.frame_peer((-1, 1)[side]),
        )

    taps_of = (
        lambda: (woa[0], wob[0], woa[1, :, 0:128]),
        lambda: (woa[1, :, 128:256], wob[1], woa[2]),
        lambda: (wob[2], woa[3], wob[3, :, 0:128]),
        lambda: (wqa[3], wqb[3]),
    )

    def times(a, t):
        return jnp.concatenate(
            [jnp.dot(a, w, preferred_element_type=F32) for w in taps_of[t]()], axis=1
        )

    def add(c):
        wide = xin[c].reshape(256, C).astype(F32)
        hidden = (wide + times(mix[c], 3)).astype(BF)
        hid[c] = hidden
        split = hidden.astype(F32).reshape(16, 2, 8, C)
        for side in range(2):
            hsend[c, side] = split[:, side].reshape(128, C).astype(BF)
            halo(c, side).start()

    def convolve(c):
        for side in range(2):
            halo(c, side).wait_recv()
        wide = hid[c].astype(F32)
        split = wide.reshape(16, 2, 8, C)
        before = hleft[c].astype(F32).reshape(16, 8, C)
        after = hright[c].astype(F32).reshape(16, 8, C)
        before = jnp.where(h.frame == 0, 0.0, before)
        after = jnp.where(h.frame == 31, 0.0, after)
        taps = (
            jnp.stack([before, split[:, 0]], axis=1).reshape(256, C).astype(BF),
            hid[c],
            jnp.stack([split[:, 1], after], axis=1).reshape(256, C).astype(BF),
        )
        for t in range(3):
            wide = wide + times(taps[t], t)
        outb[c] = wide.astype(BF).reshape(16, 16, C)
        for i in range(15):
            send_out(c, i).start()
        back[c, h.view] = outb[c, h.view]

    def send_out(c, i):
        v, device = h.view_peer(*PEERS[i])
        return remote(
            outb.at[c, v], back.at[c, h.view], out_s.at[c, i], out_r.at[c, i], device
        )

    project(0)
    advance(soa, sob)
    for k in range(5):
        attend(0, k)
    add(0)
    advance(sob)
    project(1)
    for k in range(5):
        attend(1, k)
    add(1)
    oa.arrive()
    ob.arrive()
    convolve(0)
    convolve(1)

    for g in (qa, qb, oa, ob):
        g.drain()
    for t in range(2):
        for x in range(XS):
            @pl.when(jnp.logical_not(mine & (h.x == x)))
            def _():
                shard(t, x).wait_send()
    for c in range(2):
        for side in range(2):
            halo(c, side).wait_send()
        for i in range(15):
            send_in(c, i).wait_send()
    for c in range(2):
        for i in range(15):
            send_out(c, i).wait_recv()
    both = [back[c].astype(F32).reshape(16, 2, 8, C) for c in range(2)]
    for f in range(2):
        out[0, f] = jnp.stack([b[:, f] for b in both], axis=1).reshape(PIX, C).astype(BF)
    for c in range(2):
        for i in range(15):
            send_out(c, i).wait_send()


def per_device(latents, norm_gain, qkv_weight, out_weight, conv_weight, view_slope):
    vmem = pl.BlockSpec(memory_space=pltpu.VMEM)
    dma = pltpu.SemaphoreType.DMA
    scratch = [
        pltpu.VMEM((32, 16, C), BF),
        pltpu.VMEM((2, 16, 16, C), BF),
        pltpu.VMEM((2, 16, 16, C), BF),
        pltpu.VMEM((2, 16, 16, C), BF),
        pltpu.VMEM((256, 256), F32),
        pltpu.VMEM((XS, C, SPLIT), BF),
        pltpu.VMEM((XS, C, QW - SPLIT), BF),
        pltpu.VMEM((XS, C, SPLIT), BF),
        pltpu.VMEM((XS, C, OW - SPLIT), BF),
        pltpu.VMEM((XS, 32, QW), BF),
        pltpu.VMEM((XS, 32, OW), BF),
        pltpu.VMEM((4, 32, QW), BF),
        pltpu.VMEM((4, 32, OW), BF),
        pltpu.VMEM((ROWS, QW), F32),
        pltpu.VMEM((2, 256, 3 * C), BF),
        pltpu.VMEM((2, 256, C), BF),
        pltpu.VMEM((2, 256, C), BF),
        pltpu.VMEM((2, 2, 128, C), BF),
        pltpu.VMEM((2, 128, C), BF),
        pltpu.VMEM((2, 128, C), BF),
        dma((2, 15)), dma((2, 15)), dma((2, 15)), dma((2, 15)),
        dma((2, 2)), dma((2, 2)), dma((2, 4)), dma((2, 4)),
    ]
    for _ in range(4):
        scratch += Gather.sems()
    return pl.pallas_call(
        kernel,
        out_shape=jax.ShapeDtypeStruct(latents.shape, latents.dtype),
        in_specs=[vmem] * 5 + [pl.BlockSpec(memory_space=pltpu.SMEM)],
        out_specs=vmem,
        scratch_shapes=scratch,
        compiler_params=pltpu.CompilerParams(
            collective_id=0, has_side_effects=True, vmem_limit_bytes=56 * 1024 * 1024
        ),
        cost_estimate=pl.CostEstimate(
            flops=4 * 10**9, bytes_accessed=2 * 10**6, transcendentals=10**6
        ),
    )(latents, norm_gain, qkv_weight, out_weight, conv_weight, view_slope)


def solution(mesh):
    in_specs = (
        P("view", "frame", None, None),
        P(),
        P("frame", None),
        P("frame", None),
        P(None, "frame", None),
        P(),
    )
    return jax.shard_map(
        per_device,
        mesh=mesh,
        in_specs=in_specs,
        out_specs=P("view", "frame", None, None),
        check_vma=False,
    )
```
